256 devices in a mesh: dp: 32 (over z, y_hi, core), tensor: 8 (over x, y_lo).
Axes of the slice: x: 4, y: 4 (y_hi: 2, y_lo: 2; y = y_hi * 2 + y_lo), z: 8, core: 2. Of those that a mesh axis runs over, the one named last changes fastest.
Arguments:
- inputs: bfloat16 [2048, 8192], P('tensor', 'dp'), may hold values from -6 to 6
- gate_pre: bfloat16 [2048, 14336], P('dp', 'tensor'), may hold values from -8 to 8
- up_pre: bfloat16 [2048, 14336], P('dp', 'tensor'), may hold values from -6 to 6
- hidden_grad: bfloat16 [2048, 14336], P('dp', 'tensor'), may hold values from -6 to 6
- gate_weight: bfloat16 [8192, 14336], P('dp', 'tensor'), may hold values from -0.046875 to 0.046875
- up_weight: bfloat16 [8192, 14336], P('dp', 'tensor'), may hold values from -0.046875 to 0.046875
Outputs:
- input_grad: bfloat16 [2048, 8192], P('tensor', 'dp')
- gate_wgrad: float32 [8192, 14336], P('dp', 'tensor')
- up_wgrad: float32 [8192, 14336], P('dp', 'tensor')
The draws below stay inside these ranges and needn't reach their ends.
All inputs are finite; a program needn't handle non-finite values.
Results may differ from the reference program's by a relative error of at most 0.017.
Values may be sent and summed in bfloat16 or wider, within the bound.
A program may use at most 64 MiB of HBM per device.

```python
import math
import jax
import jax.numpy as jnp

D = 8192
FF = 14336
TOKENS = 2048
N_TENSOR = 8


def spiked(entries, rng, source, target, shards_of, factor):
    def block_of(axis_at):
        return (jnp.arange(entries.shape[axis_at]) // (entries.shape[axis_at] // shards_of)).reshape((-1,) + (1,) * (entries.ndim - 1 - axis_at))

    near = jax.random.permutation(rng, shards_of)[block_of(target)]
    second = (block_of(target) + shards_of // 2) % shards_of
    return jnp.where((block_of(source) == near) | (block_of(source) == second), factor * entries, entries)


def block_scale(own_key, shape, split, low, largest):
    def one(position, parts):
        draws = jax.random.uniform(jax.random.fold_in(jax.random.fold_in(own_key, 6), position), (parts,), jnp.float32, low / len(split), largest / len(split))
        return jnp.repeat(jnp.exp(draws), shape[position] // parts).reshape((-1,) + (1,) * (len(shape) - position - 1))

    gain = one(*split[0])
    for cut in split[1:]:
        gain = gain * one(*cut)
    return gain


def centred(own_key, dims, scale, bound, cuts=(), dtype=jnp.bfloat16):
    drawn = scale * jax.random.normal(own_key, dims, jnp.float32)
    if cuts:
        drawn = drawn * block_scale(own_key, dims, cuts, -0.22, 0.18)
    return jnp.clip(drawn, -bound, bound).astype(dtype)


def gaussian_with(key, shape, width, limit, split, heavy, held_as=jnp.bfloat16):
    values = width * jax.random.normal(key, shape, jnp.float32)
    if split:
        values = values * block_scale(key, shape, split, -0.22, 0.18)
    return jnp.clip(spiked(values, jax.random.fold_in(key, 3), *heavy), -limit, limit).astype(held_as)


def setup_inputs(seed: int = 0) -> dict:
    streams_of = jax.random.split(jax.random.key(seed), 7)
    inputs = centred(streams_of[0], (TOKENS, D), 1.0, 6.0, ((0, 8), (1, 32)))
    gate_pre = centred(streams_of[1], (TOKENS, FF), 2.0, 8.0, ((0, 32), (1, 8)))
    up_pre = centred(streams_of[2], (TOKENS, FF), 1.0, 6.0, ((0, 32), (1, 8)))
    hidden_grad = gaussian_with(streams_of[3], (TOKENS, FF), 1.0, 6.0, ((0, 32), (1, 8)), (1, 0, 32, 2.75))
    gate_weight = centred(streams_of[4], (D, FF), FF ** -0.5, 0.046875, ((0, 32), (1, 8)))
    up_weight = centred(streams_of[5], (D, FF), FF ** -0.5, 0.046875, ((0, 32), (1, 8)))
    return dict(inputs=inputs, gate_pre=gate_pre, up_pre=up_pre, hidden_grad=hidden_grad, gate_weight=gate_weight, up_weight=up_weight)


def reference(inputs, gate_pre, up_pre, hidden_grad, gate_weight, up_weight):
    gate_value = gate_pre.astype(jnp.float32)
    up_value = up_pre.astype(jnp.float32)
    grad_value = hidden_grad.astype(jnp.float32)
    sigmoid_gate = 1.0 / (1.0 + jnp.exp(-gate_value))
    up_grad = (grad_value * gate_value * sigmoid_gate).astype(jnp.bfloat16)
    gate_grad = (grad_value * up_value * sigmoid_gate * (1.0 + gate_value * (1.0 - sigmoid_gate))).astype(jnp.bfloat16)
    grad_scale = 1.0 / math.sqrt(TOKENS)
    gate_wgrad = jnp.dot(inputs.T, gate_grad, preferred_element_type=jnp.float32) * grad_scale
    up_wgrad = jnp.dot(inputs.T, up_grad, preferred_element_type=jnp.float32) * grad_scale
    block_width = FF // N_TENSOR
    input_grad = jnp.zeros((TOKENS, D), jnp.float32)
    for block in range(N_TENSOR):
        lower = block * block_width
        upper = lower + block_width
        part_sum = jnp.dot(gate_grad[:, lower:upper], gate_weight[:, lower:upper].T, preferred_element_type=jnp.float32)
        part_sum = part_sum + jnp.dot(up_grad[:, lower:upper], up_weight[:, lower:upper].T, preferred_element_type=jnp.float32)
        input_grad = input_grad + part_sum.astype(jnp.bfloat16).astype(jnp.float32)
    return (input_grad.astype(jnp.bfloat16), gate_wgrad, up_wgrad)
```

```python
import functools
import math

import jax
import jax.numpy as jnp
from jax import lax
from jax.experimental import pallas as pl
from jax.experimental.pallas import tpu as pltpu
from jax.sharding import PartitionSpec as P

MESH = pl.DeviceIdType.MESH
ROWS = 64
GROUP = 256
HID = 1792
FEAT = 256
NZ = 8
NX = 4
GATE, UP = 0, 1
SCALE = 1.0 / math.sqrt(2048)
OFFS = (0, -1, 1, -2, 2, -3, 3, 4)


def kernel(
    inputs, gate_pre, up_pre, hidden_grad, gate_weight, up_weight,
    igrad_out, gate_out, up_out,
    grads, xs, xt, w, wt, acc, part, part_b, rx, ry, sy, fin, pre,
    loc, z_s, z_r, f_s, f_r, y_s, y_r, c_s, c_r, x_s, x_r, g_s, g_r, h_s, h_r, out_sem,
):
    dp, tensor = lax.axis_index("dp"), lax.axis_index("tensor")
    z, yh, c = dp // 4, (dp // 2) % 2, dp % 2
    x, yl = tensor // 2, tensor % 2

    def at_z(step):
        return {"dp": ((z + step + NZ) % NZ) * 4 + yh * 2 + c, "tensor": tensor}

    opposite = {"dp": z * 4 + (1 - yh) * 2 + c, "tensor": tensor}
    sibling = {"dp": z * 4 + yh * 2 + (1 - c), "tensor": tensor}
    partner = {"dp": dp, "tensor": x * 2 + (1 - yl)}

    def at_x(step):
        return {"dp": dp, "tensor": ((x + step) % NX) * 2 + yl}

    def group(off):
        return (z + off + NZ) % NZ

    own_rows = pl.multiple_of(yh * 128 + c * ROWS, ROWS)
    opp_rows = pl.multiple_of((1 - yh) * 128 + c * ROWS, ROWS)

    def block(kind, src_z, far):
        return grads.at[kind, src_z, pl.ds(opp_rows if far else own_rows, ROWS), :]

    def remote(src, dst, s, r, dev):
        return pltpu.make_async_remote_copy(
            src_ref=src, dst_ref=dst, send_sem=s, recv_sem=r, device_id=dev, device_id_type=MESH
        )

    STREAM = ((GATE, 0), (UP, 0), (UP, 1))

    def z_copy(way, stream, hop):
        kind, far = STREAM[stream]
        step = 1 - 2 * way
        b = block(kind, group(-step * hop), far)
        return remote(b, b, z_s.at[way, stream, hop], z_r.at[way, stream, hop], at_z(step))

    def far_copy(stream):
        kind, far = STREAM[stream]
        step = 1 - 2 * c
        b = block(kind, group(-3 * step), far)
        return remote(b, b, f_s.at[stream], f_r.at[stream], at_z(step))

    def y_copy(kind, off):
        slot = NZ if kind == UP else off % NZ
        b = block(kind, group(off), 0)
        return remote(b, b, y_s.at[slot], y_r.at[slot], opposite)

    def c_copy(kind, far, off):
        b = block(kind, group(off), far)
        i = off % NZ
        return remote(b, b, c_s.at[kind, far, i], c_r.at[kind, far, i], sibling)

    def x_copy(slot):
        if slot == 0:
            return remote(inputs, xs.at[tensor], x_s.at[0], x_r.at[0], partner)
        if slot <= 3:
            return remote(inputs, xs.at[tensor], x_s.at[slot], x_r.at[slot], at_x(slot))
        b = xs.at[x * 2 + (1 - yl)]
        return remote(b, b, x_s.at[slot], x_r.at[slot], at_x(slot - 3))

    pre_loads = [
        pltpu.make_async_copy(ref, pre.at[i], loc.at[i])
        for i, ref in enumerate((gate_pre, up_pre, hidden_grad))
    ]
    w_loads = [
        pltpu.make_async_copy(ref, w.at[i], loc.at[3 + i])
        for i, ref in enumerate((gate_weight, up_weight))
    ]
    x_load = pltpu.make_async_copy(inputs, xs.at[tensor], loc.at[5])
    for cp in pre_loads + w_loads + [x_load]:
        cp.start()

    barrier = pltpu.get_barrier_semaphore()
    peers = [at_z(1), at_z(-1), opposite, sibling, partner, at_x(1), at_x(2), at_x(3)]
    for peer in peers:
        pl.semaphore_signal(barrier, inc=1, device_id=peer, device_id_type=MESH)

    for cp in pre_loads:
        cp.wait()

    def elementwise(i, _):
        cols = pl.ds(pl.multiple_of(i * 256, 256), 256)
        gate_value = pre[0, :, cols].astype(jnp.float32)
        up_value = pre[1, :, cols].astype(jnp.float32)
        grad_value = pre[2, :, cols].astype(jnp.float32)
        sig = 1.0 / (1.0 + jnp.exp(-gate_value))
        grads[UP, z, pl.ds(own_rows, ROWS), cols] = (grad_value * gate_value * sig).astype(jnp.bfloat16)
        grads[GATE, z, pl.ds(own_rows, ROWS), cols] = (
            grad_value * up_value * sig * (1.0 + gate_value * (1.0 - sig))
        ).astype(jnp.bfloat16)
        return 0

    lax.fori_loop(0, HID // 256, elementwise, 0)
    pl.semaphore_wait(barrier, len(peers))

    started = []

    def go(cp):
        cp.start()
        started.append(cp)

    def arrive_z(stream, hop):
        kind, far = STREAM[stream]
        for way in (0, 1):
            z_copy(way, stream, hop).wait_recv()
            if hop < 2:
                go(z_copy(way, stream, hop + 1))
        if hop == 2:
            go(far_copy(stream))
        for off in (-(hop + 1), hop + 1):
            if kind == GATE:
                go(y_copy(GATE, off))
            go(c_copy(kind, far, off))

    def arrive_far(stream):
        kind, far = STREAM[stream]
        far_copy(stream).wait_recv()
        if kind == GATE:
            go(y_copy(GATE, 4))
        go(c_copy(kind, far, 4))

    def arrive_y(off):
        y_copy(GATE, off).wait_recv()
        go(c_copy(GATE, 1, off))

    def from_sibling(kind, off):
        for far in (0, 1):
            c_copy(kind, far, off).wait_recv()

    def wgrad(kind, off):
        g = group(off)
        for half in (0, 1):
            cols = pl.ds(half * 896, 896)
            prod = jnp.dot(xt[g], grads[kind, g, :, cols], preferred_element_type=jnp.float32)
            if off != 0:
                prod = acc[kind, :, cols] + prod
            if off == 4:
                prod = prod * SCALE
            acc[kind, :, cols] = prod

    def igrad(kind, off):
        g = group(off)
        prod = jnp.dot(grads[kind, g], wt[kind], preferred_element_type=jnp.float32)
        if kind == GATE:
            part[g] = prod
        else:
            part_b[g] = (part[g] + prod).astype(jnp.bfloat16)

    def scatter(off):
        g = group(off)
        gx, gl = g // 2, g % 2
        i = off % NZ
        slot = (x - gx + NX) % NX - 1

        def copy():
            return remote(
                part_b.at[g], rx.at[gl, slot], g_s.at[i], g_r.at[gl, slot],
                {"dp": dp, "tensor": gx * 2 + yl},
            )

        return x != gx, copy

    def send_part(off):
        cond, copy = scatter(off)
        pl.when(cond)(lambda: copy().start())

    for way in (0, 1):
        go(z_copy(way, 0, 0))
    go(y_copy(UP, 0))
    for way in (0, 1):
        go(z_copy(way, 1, 0))
    go(c_copy(UP, 0, 0))
    go(c_copy(GATE, 0, 0))
    go(x_copy(0))
    go(y_copy(GATE, 0))
    for slot in (1, 2, 3):
        go(x_copy(slot))

    for cp in w_loads:
        cp.wait()

    def flip_w(i, _):
        cols = pl.ds(pl.multiple_of(i * 256, 256), 256)
        for kind in (GATE, UP):
            wt[kind, cols, :] = w[kind, :, cols].T
        return 0

    x_copy(0).wait_recv()
    for slot in (4, 5, 6):
        go(x_copy(slot))
    lax.fori_loop(0, HID // 256, flip_w, 0)

    arrive_z(0, 0)
    y_copy(UP, 0).wait_recv()
    for way in (0, 1):
        go(z_copy(way, 2, 0))
    go(c_copy(UP, 1, 0))
    arrive_z(1, 0)
    arrive_y(0)

    x_load.wait()
    for slot in range(1, 7):
        x_copy(slot).wait_recv()

    def flip_x(i, _):
        xt[i] = xs[i].T
        return 0

    lax.fori_loop(0, NZ, flip_x, 0)

    def do(kind, off):
        from_sibling(kind, off)
        igrad(kind, off)
        if kind == UP:
            send_part(off)
        wgrad(kind, off)

    do(GATE, 0)
    do(UP, 0)
    arrive_z(0, 1)
    arrive_y(-1)
    arrive_z(2, 0)
    arrive_y(1)
    do(GATE, -1)
    do(GATE, 1)
    arrive_z(1, 1)
    arrive_y(-2)
    do(UP, -1)
    do(UP, 1)
    arrive_z(0, 2)
    arrive_y(2)
    do(GATE, -2)
    do(GATE, 2)
    arrive_z(2, 1)
    arrive_y(-3)
    do(UP, -2)
    do(UP, 2)
    arrive_z(1, 2)
    arrive_y(3)
    do(GATE, -3)
    do(GATE, 3)
    arrive_far(0)
    arrive_z(2, 2)
    do(UP, -3)
    do(UP, 3)
    arrive_far(1)
    arrive_y(4)
    do(GATE, 4)
    gate_store = pltpu.make_async_copy(acc.at[GATE], gate_out, out_sem.at[0])
    gate_store.start()
    arrive_far(2)
    do(UP, 4)
    up_store = pltpu.make_async_copy(acc.at[UP], up_out, out_sem.at[1])
    up_store.start()

    def x_sum(gl):
        total = part_b[x * 2 + gl].astype(jnp.float32)
        for slot in range(3):
            remote(
                part_b.at[0], rx.at[gl, slot], g_s.at[0], g_r.at[gl, slot], sibling
            ).wait_recv()
            total = total + rx[gl, slot].astype(jnp.float32)
        return total

    sy[...] = x_sum(1 - yl).astype(jnp.bfloat16)
    y_part = remote(sy, ry, h_s, h_r, partner)
    y_part.start()
    total = x_sum(yl)
    y_part.wait_recv()
    fin[...] = (total + ry[...].astype(jnp.float32)).astype(jnp.bfloat16)
    fin_store = pltpu.make_async_copy(fin, igrad_out, out_sem.at[2])
    fin_store.start()

    for cp in started:
        cp.wait_send()
    for off in OFFS:
        cond, copy = scatter(off)
        pl.when(cond)(lambda: copy().wait_send())
    y_part.wait_send()
    for cp in (gate_store, up_store, fin_store):
        cp.wait()


def per_device(*args):
    bf16, f32 = jnp.bfloat16, jnp.float32
    dma = pltpu.SemaphoreType.DMA
    hbm = pl.BlockSpec(memory_space=pl.ANY)
    return tuple(
        pl.pallas_call(
            kernel,
            out_shape=(
                jax.ShapeDtypeStruct((GROUP, FEAT), bf16),
                jax.ShapeDtypeStruct((FEAT, HID), f32),
                jax.ShapeDtypeStruct((FEAT, HID), f32),
            ),
            in_specs=[hbm] * 6,
            out_specs=(hbm,) * 3,
            scratch_shapes=[
                pltpu.VMEM((2, NZ, GROUP, HID), bf16),
                pltpu.VMEM((NZ, GROUP, FEAT), bf16),
                pltpu.VMEM((NZ, FEAT, GROUP), bf16),
                pltpu.VMEM((2, FEAT, HID), bf16),
                pltpu.VMEM((2, HID, FEAT), bf16),
                pltpu.VMEM((2, FEAT, HID), f32),
                pltpu.VMEM((NZ, GROUP, FEAT), f32),
                pltpu.VMEM((NZ, GROUP, FEAT), bf16),
                pltpu.VMEM((2, 3, GROUP, FEAT), bf16),
                pltpu.VMEM((GROUP, FEAT), bf16),
                pltpu.VMEM((GROUP, FEAT), bf16),
                pltpu.VMEM((GROUP, FEAT), bf16),
                pltpu.VMEM((3, ROWS, HID), bf16),
                dma((6,)),
                dma((2, 3, 3)), dma((2, 3, 3)),
                dma((3,)), dma((3,)),
                dma((NZ + 1,)), dma((NZ + 1,)),
                dma((2, 2, NZ)), dma((2, 2, NZ)),
                dma((7,)), dma((7,)),
                dma((NZ,)), dma((2, 3)),
                dma, dma,
                dma((3,)),
            ],
            compiler_params=pltpu.CompilerParams(
                collective_id=0, has_side_effects=True, vmem_limit_bytes=48 * 2**20
            ),
            cost_estimate=pl.CostEstimate(flops=7516192768, bytes_accessed=8 * 2**20, transcendentals=0),
            name="swiglu_bwd",
        )(*args)
    )


def solution(mesh):
    in_specs = (
        P("tensor", "dp"),
        P("dp", "tensor"),
        P("dp", "tensor"),
        P("dp", "tensor"),
        P("dp", "tensor"),
        P("dp", "tensor"),
    )
    out_specs = (P("tensor", "dp"), P("dp", "tensor"), P("dp", "tensor"))
    return jax.shard_map(
        per_device, mesh=mesh, in_specs=in_specs, out_specs=out_specs, check_vma=False
    )
```

```python
import functools
import math

import jax
import jax.numpy as jnp
from jax import lax
from jax.experimental import pallas as pl
from jax.experimental.pallas import tpu as pltpu
from jax.sharding import PartitionSpec as P

MESH = pl.DeviceIdType.MESH
ROWS = 64
GROUP = 256
HID = 1792
FEAT = 256
NZ = 8
NX = 4
GATE, UP = 0, 1
VMEM_BYTES = 56 * 2**20
SCALE = 1.0 / math.sqrt(2048)
OFFS = (0, -1, 1, -2, 2, -3, 3, 4)


def kernel(
    inputs, gate_pre, up_pre, hidden_grad, gate_weight, up_weight,
    igrad_out, gate_acc, up_acc,
    grads, xs, xt, w, wt, part, part_b, rx, ry, sy, pre,
    loc, z_s, z_r, f_s, f_r, y_s, y_r, c_s, c_r, x_s, x_r, g_s, g_r, h_s, h_r,
):
    dp, tensor = lax.axis_index("dp"), lax.axis_index("tensor")
    z, yh, c = dp // 4, (dp // 2) % 2, dp % 2
    x, yl = tensor // 2, tensor % 2

    def at_z(step):
        return {"dp": ((z + step + NZ) % NZ) * 4 + yh * 2 + c, "tensor": tensor}

    opposite = {"dp": z * 4 + (1 - yh) * 2 + c, "tensor": tensor}
    sibling = {"dp": z * 4 + yh * 2 + (1 - c), "tensor": tensor}
    partner = {"dp": dp, "tensor": x * 2 + (1 - yl)}

    def at_x(step):
        return {"dp": dp, "tensor": ((x + step) % NX) * 2 + yl}

    def group(off):
        return (z + off + NZ) % NZ

    own_rows = pl.multiple_of(yh * 128 + c * ROWS, ROWS)
    opp_rows = pl.multiple_of((1 - yh) * 128 + c * ROWS, ROWS)

    def block(kind, src_z, far):
        return grads.at[kind, src_z, pl.ds(opp_rows if far else own_rows, ROWS), :]

    def remote(src, dst, s, r, dev):
        return pltpu.make_async_remote_copy(
            src_ref=src, dst_ref=dst, send_sem=s, recv_sem=r, device_id=dev, device_id_type=MESH
        )

    STREAM = ((GATE, 0), (UP, 0), (UP, 1))

    def z_copy(way, stream, hop):
        kind, far = STREAM[stream]
        step = 1 - 2 * way
        b = block(kind, group(-step * hop), far)
        return remote(b, b, z_s.at[way, stream, hop], z_r.at[way, stream, hop], at_z(step))

    def far_copy(stream):
        kind, far = STREAM[stream]
        step = 1 - 2 * c
        b = block(kind, group(-3 * step), far)
        return remote(b, b, f_s.at[stream], f_r.at[stream], at_z(step))

    def y_copy(kind, off):
        slot = NZ if kind == UP else off % NZ
        b = block(kind, group(off), 0)
        return remote(b, b, y_s.at[slot], y_r.at[slot], opposite)

    def c_copy(kind, far, off):
        b = block(kind, group(off), far)
        i = off % NZ
        return remote(b, b, c_s.at[kind, far, i], c_r.at[kind, far, i], sibling)

    def x_copy(slot):
        if slot == 0:
            return remote(inputs, xs.at[tensor], x_s.at[0], x_r.at[0], partner)
        if slot <= 3:
            return remote(inputs, xs.at[tensor], x_s.at[slot], x_r.at[slot], at_x(slot))
        b = xs.at[x * 2 + (1 - yl)]
        return remote(b, b, x_s.at[slot], x_r.at[slot], at_x(slot - 3))

    pre_loads = [
        pltpu.make_async_copy(ref, pre.at[i], loc.at[i])
        for i, ref in enumerate((gate_pre, up_pre, hidden_grad))
    ]
    w_loads = [
        pltpu.make_async_copy(ref, w.at[i], loc.at[3 + i])
        for i, ref in enumerate((gate_weight, up_weight))
    ]
    x_load = pltpu.make_async_copy(inputs, xs.at[tensor], loc.at[5])
    for cp in pre_loads + w_loads + [x_load]:
        cp.start()

    barrier = pltpu.get_barrier_semaphore()
    peers = [at_z(1), at_z(-1), opposite, sibling, partner, at_x(1), at_x(2), at_x(3)]
    for peer in peers:
        pl.semaphore_signal(barrier, inc=1, device_id=peer, device_id_type=MESH)

    for cp in pre_loads:
        cp.wait()

    def elementwise(i, _):
        cols = pl.ds(pl.multiple_of(i * 256, 256), 256)
        gate_value = pre[0, :, cols].astype(jnp.float32)
        up_value = pre[1, :, cols].astype(jnp.float32)
        grad_value = pre[2, :, cols].astype(jnp.float32)
        sig = 1.0 / (1.0 + jnp.exp(-gate_value))
        grads[UP, z, pl.ds(own_rows, ROWS), cols] = (grad_value * gate_value * sig).astype(jnp.bfloat16)
        grads[GATE, z, pl.ds(own_rows, ROWS), cols] = (
            grad_value * up_value * sig * (1.0 + gate_value * (1.0 - sig))
        ).astype(jnp.bfloat16)
        return 0

    lax.fori_loop(0, HID // 256, elementwise, 0)
    pl.semaphore_wait(barrier, len(peers))

    started = []

    def go(cp):
        cp.start()
        started.append(cp)

    def arrive_z(stream, hop):
        kind, far = STREAM[stream]
        for way in (0, 1):
            z_copy(way, stream, hop).wait_recv()
            if hop < 2:
                go(z_copy(way, stream, hop + 1))
        if hop == 2:
            go(far_copy(stream))
        for off in (-(hop + 1), hop + 1):
            if kind == GATE:
                go(y_copy(GATE, off))
            go(c_copy(kind, far, off))

    def arrive_far(stream):
        kind, far = STREAM[stream]
        far_copy(stream).wait_recv()
        if kind == GATE:
            go(y_copy(GATE, 4))
        go(c_copy(kind, far, 4))

    def arrive_y(off):
        y_copy(GATE, off).wait_recv()
        go(c_copy(GATE, 1, off))

    def from_sibling(kind, far, off):
        c_copy(kind, far, off).wait_recv()

    def wgrad(kind, off):
        g = group(off)
        acc = (gate_acc, up_acc)[kind]
        for half in (0, 1):
            cols = pl.ds(half * 896, 896)
            prod = jnp.dot(xt[g], grads[kind, g, :, cols], preferred_element_type=jnp.float32)
            if off != 0:
                prod = acc[:, cols] + prod
            if off == 4:
                prod = prod * SCALE
            acc[:, cols] = prod

    def igrad(kind, off):
        g = group(off)
        part[g] = jnp.dot(grads[kind, g], wt[kind], preferred_element_type=jnp.float32)

    def finish(off, far):
        g = group(off)
        rows = pl.ds(pl.multiple_of((1 - yh if far else yh) * 128, 128), 128)
        prod = jnp.dot(grads[UP, g, rows, :], wt[UP], preferred_element_type=jnp.float32)
        part_b[g, rows, :] = (part[g, rows, :] + prod).astype(jnp.bfloat16)
        cond, copy = scatter(off, far)
        pl.when(cond)(lambda: copy().start())

    def scatter(off, far):
        g = group(off)
        gx, gl = g // 2, g % 2
        i = off % NZ
        slot = (x - gx + NX) % NX - 1
        rows = pl.ds(pl.multiple_of((1 - yh if far else yh) * 128, 128), 128)

        def copy():
            return remote(
                part_b.at[g, rows, :], rx.at[gl, slot, rows, :], g_s.at[i, far], g_r.at[gl, slot, far],
                {"dp": dp, "tensor": gx * 2 + yl},
            )

        return x != gx, copy

    for way in (0, 1):
        go(z_copy(way, 0, 0))
    go(y_copy(UP, 0))
    for way in (0, 1):
        go(z_copy(way, 1, 0))
    go(c_copy(UP, 0, 0))
    go(c_copy(GATE, 0, 0))
    go(x_copy(0))
    go(y_copy(GATE, 0))
    for slot in (1, 2, 3):
        go(x_copy(slot))

    for cp in w_loads:
        cp.wait()

    def flip_w(i, _):
        cols = pl.ds(pl.multiple_of(i * 256, 256), 256)
        for kind in (GATE, UP):
            wt[kind, cols, :] = w[kind, :, cols].T
        return 0

    lax.fori_loop(0, HID // 256, flip_w, 0)

    arrive_z(0, 0)
    y_copy(UP, 0).wait_recv()
    for way in (0, 1):
        go(z_copy(way, 2, 0))
    go(c_copy(UP, 1, 0))
    x_copy(0).wait_recv()
    for slot in (4, 5, 6):
        go(x_copy(slot))
    arrive_z(1, 0)

    x_load.wait()
    for slot in range(1, 7):
        x_copy(slot).wait_recv()

    def flip_x(i, _):
        xt[i] = xs[i].T
        return 0

    lax.fori_loop(0, NZ, flip_x, 0)

    def do(kind, off):
        if kind == GATE:
            from_sibling(GATE, 0, off)
            from_sibling(GATE, 1, off)
            igrad(GATE, off)
        else:
            for far in (0, 1):
                from_sibling(UP, far, off)
                finish(off, far)
        wgrad(kind, off)

    arrive_y(0)
    arrive_z(0, 1)
    do(GATE, 0)
    do(UP, 0)
    arrive_y(-1)
    arrive_z(2, 0)
    do(GATE, -1)
    arrive_y(1)
    arrive_z(1, 1)
    do(UP, -1)
    do(GATE, 1)
    do(UP, 1)
    arrive_y(-2)
    arrive_z(0, 2)
    do(GATE, -2)
    arrive_y(2)
    arrive_z(2, 1)
    do(GATE, 2)
    arrive_y(-3)
    arrive_z(1, 2)
    do(UP, -2)
    arrive_far(0)
    do(UP, 2)
    arrive_y(3)
    do(GATE, -3)
    do(GATE, 3)
    arrive_z(2, 2)
    do(UP, -3)
    arrive_y(4)
    do(UP, 3)
    arrive_far(1)
    do(GATE, 4)
    from_sibling(UP, 0, 4)
    finish(4, 0)
    arrive_far(2)
    from_sibling(UP, 1, 4)
    finish(4, 1)
    wgrad(UP, 4)

    def half(far):
        return pl.ds(pl.multiple_of((1 - yh if far else yh) * 128, 128), 128)

    def x_sum(gl, far):
        rows = half(far)
        total = part_b[x * 2 + gl, rows, :].astype(jnp.float32)
        for slot in range(3):
            b = rx.at[gl, slot, rows, :]
            remote(b, b, g_s.at[0, 0], g_r.at[gl, slot, far], sibling).wait_recv()
            total = total + rx[gl, slot, rows, :].astype(jnp.float32)
        return total

    def y_part(far):
        rows = half(far)
        return remote(sy.at[rows, :], ry.at[rows, :], h_s.at[far], h_r.at[far], partner)

    def sum_half(far):
        rows = half(far)
        sy[rows, :] = x_sum(1 - yl, far).astype(jnp.bfloat16)
        y_part(far).start()
        part[0, rows, :] = x_sum(yl, far)

    def end_half(far):
        rows = half(far)
        y_part(far).wait_recv()
        igrad_out[rows, :] = (part[0, rows, :] + ry[rows, :].astype(jnp.float32)).astype(jnp.bfloat16)

    sum_half(0)
    sum_half(1)
    end_half(0)
    end_half(1)

    for cp in started:
        cp.wait_send()
    for off in OFFS:
        for far in (0, 1):
            cond, copy = scatter(off, far)
            pl.when(cond)(lambda: copy().wait_send())
    for far in (0, 1):
        y_part(far).wait_send()


def write_out(*refs):
    n = len(refs) // 2
    sem = refs[-1]
    copies = [pltpu.make_async_copy(refs[i], refs[n + i], sem.at[i]) for i in range(n)]
    for cp in copies:
        cp.start()
    for cp in copies:
        cp.wait()


def per_device(*args):
    bf16, f32 = jnp.bfloat16, jnp.float32
    dma = pltpu.SemaphoreType.DMA
    hbm = pl.BlockSpec(memory_space=pl.ANY)
    vmem = pl.BlockSpec(memory_space=pltpu.VMEM)
    outs = (((GROUP, FEAT), bf16), ((FEAT, HID), f32), ((FEAT, HID), f32))
    held = pl.pallas_call(
        kernel,
        out_shape=tuple(pltpu.VMEM(*o) for o in outs),
        in_specs=[hbm] * 6,
        out_specs=(vmem,) * 3,
        scratch_shapes=[
            pltpu.VMEM((2, NZ, GROUP, HID), bf16),
            pltpu.VMEM((NZ, GROUP, FEAT), bf16),
            pltpu.VMEM((NZ, FEAT, GROUP), bf16),
            pltpu.VMEM((2, FEAT, HID), bf16),
            pltpu.VMEM((2, HID, FEAT), bf16),
            pltpu.VMEM((NZ, GROUP, FEAT), f32),
            pltpu.VMEM((NZ, GROUP, FEAT), bf16),
            pltpu.VMEM((2, 3, GROUP, FEAT), bf16),
            pltpu.VMEM((GROUP, FEAT), bf16),
            pltpu.VMEM((GROUP, FEAT), bf16),
            pltpu.VMEM((3, ROWS, HID), bf16),
            dma((6,)),
            dma((2, 3, 3)), dma((2, 3, 3)),
            dma((3,)), dma((3,)),
            dma((NZ + 1,)), dma((NZ + 1,)),
            dma((2, 2, NZ)), dma((2, 2, NZ)),
            dma((7,)), dma((7,)),
            dma((NZ, 2)), dma((2, 3, 2)),
            dma((2,)), dma((2,)),
        ],
        compiler_params=pltpu.CompilerParams(
            collective_id=0, has_side_effects=True, vmem_limit_bytes=VMEM_BYTES
        ),
        cost_estimate=pl.CostEstimate(flops=7516192768, bytes_accessed=8 * 2**20, transcendentals=0),
        name="swiglu_bwd",
    )(*args)
    return tuple(
        pl.pallas_call(
            write_out,
            out_shape=tuple(jax.ShapeDtypeStruct(*o) for o in outs),
            in_specs=[hbm] * 3,
            out_specs=(hbm,) * 3,
            scratch_shapes=[dma((3,))],
            compiler_params=pltpu.CompilerParams(vmem_limit_bytes=4 * 2**20),
            name="write_out",
        )(*held)
    )


def solution(mesh):
    in_specs = (
        P("tensor", "dp"),
        P("dp", "tensor"),
        P("dp", "tensor"),
        P("dp", "tensor"),
        P("dp", "tensor"),
        P("dp", "tensor"),
    )
    out_specs = (P("tensor", "dp"), P("dp", "tensor"), P("dp", "tensor"))
    return jax.shard_map(
        per_device, mesh=mesh, in_specs=in_specs, out_specs=out_specs, check_vma=False
    )
```

```python
import functools
import math

import jax
import jax.numpy as jnp
from jax import lax
from jax.experimental import pallas as pl
from jax.experimental.pallas import tpu as pltpu
from jax.sharding import PartitionSpec as P

MESH = pl.DeviceIdType.MESH
ROWS = 64
GROUP = 256
HID = 1792
FEAT = 256
NZ = 8
NX = 4
PIECE = 128 // NX
PARTS = 1
GATE, UP = 0, 1
VMEM_BYTES = 56 * 2**20
SCALE = 1.0 / math.sqrt(2048)
OFFS = (0, -1, 1, -2, 2, -3, 3, 4)


def kernel(
    inputs, gate_pre, up_pre, hidden_grad, gate_weight, up_weight,
    igrad_out, gate_acc, up_acc,
    grads, xs, xt, w, wt, part, part_b, rx, sums, fin, pre,
    loc, z_s, z_r, f_s, f_r, y_s, y_r, c_s, c_r, x_s, x_r, g_s, g_r, h_s, h_r,
):
    dp, tensor = lax.axis_index("dp"), lax.axis_index("tensor")
    z, yh, c = dp // 4, (dp // 2) % 2, dp % 2
    x, yl = tensor // 2, tensor % 2

    def at_z(step):
        return {"dp": ((z + step + NZ) % NZ) * 4 + yh * 2 + c, "tensor": tensor}

    opposite = {"dp": z * 4 + (1 - yh) * 2 + c, "tensor": tensor}
    sibling = {"dp": z * 4 + yh * 2 + (1 - c), "tensor": tensor}
    partner = {"dp": dp, "tensor": x * 2 + (1 - yl)}

    def at_x(step):
        return {"dp": dp, "tensor": ((x + step) % NX) * 2 + yl}

    def group(off):
        return (z + off + NZ) % NZ

    own_rows = pl.multiple_of(yh * 128 + c * ROWS, ROWS)
    opp_rows = pl.multiple_of((1 - yh) * 128 + c * ROWS, ROWS)

    def block(kind, src_z, far):
        return grads.at[kind, src_z, pl.ds(opp_rows if far else own_rows, ROWS), :]

    def remote(src, dst, s, r, dev):
        return pltpu.make_async_remote_copy(
            src_ref=src, dst_ref=dst, send_sem=s, recv_sem=r, device_id=dev, device_id_type=MESH
        )

    STREAM = ((GATE, 0), (UP, 0), (UP, 1))

    def z_copy(way, stream, hop):
        kind, far = STREAM[stream]
        step = 1 - 2 * way
        b = block(kind, group(-step * hop), far)
        return remote(b, b, z_s.at[way, stream, hop], z_r.at[way, stream, hop], at_z(step))

    def far_copy(stream):
        kind, far = STREAM[stream]
        step = 1 - 2 * c
        b = block(kind, group(-3 * step), far)
        return remote(b, b, f_s.at[stream], f_r.at[stream], at_z(step))

    def y_copy(kind, off):
        slot = NZ if kind == UP else off % NZ
        b = block(kind, group(off), 0)
        return remote(b, b, y_s.at[slot], y_r.at[slot], opposite)

    def c_copy(kind, far, off):
        b = block(kind, group(off), far)
        i = off % NZ
        return remote(b, b, c_s.at[kind, far, i], c_r.at[kind, far, i], sibling)

    def x_copy(slot):
        if slot == 0:
            return remote(inputs, xs.at[tensor], x_s.at[0], x_r.at[0], partner)
        if slot <= 3:
            return remote(inputs, xs.at[tensor], x_s.at[slot], x_r.at[slot], at_x(slot))
        b = xs.at[x * 2 + (1 - yl)]
        return remote(b, b, x_s.at[slot], x_r.at[slot], at_x(slot - 3))

    pre_loads = [
        pltpu.make_async_copy(ref, pre.at[i], loc.at[i])
        for i, ref in enumerate((gate_pre, up_pre, hidden_grad))
    ]
    w_loads = [
        pltpu.make_async_copy(ref, w.at[i], loc.at[3 + i])
        for i, ref in enumerate((gate_weight, up_weight))
    ]
    x_load = pltpu.make_async_copy(inputs, xs.at[tensor], loc.at[5])
    for cp in pre_loads + w_loads + [x_load]:
        cp.start()

    barrier = pltpu.get_barrier_semaphore()
    peers = [at_z(1), at_z(-1), opposite, sibling]
    peers += [{"dp": dp, "tensor": (tensor + i) % NZ} for i in range(1, NZ)]
    for peer in peers:
        pl.semaphore_signal(barrier, inc=1, device_id=peer, device_id_type=MESH)

    for cp in pre_loads:
        cp.wait()

    def elementwise(i, _):
        cols = pl.ds(pl.multiple_of(i * 256, 256), 256)
        gate_value = pre[0, :, cols].astype(jnp.float32)
        up_value = pre[1, :, cols].astype(jnp.float32)
        grad_value = pre[2, :, cols].astype(jnp.float32)
        sig = 1.0 / (1.0 + jnp.exp(-gate_value))
        grads[UP, z, pl.ds(own_rows, ROWS), cols] = (grad_value * gate_value * sig).astype(jnp.bfloat16)
        grads[GATE, z, pl.ds(own_rows, ROWS), cols] = (
            grad_value * up_value * sig * (1.0 + gate_value * (1.0 - sig))
        ).astype(jnp.bfloat16)
        return 0

    lax.fori_loop(0, HID // 256, elementwise, 0)
    pl.semaphore_wait(barrier, len(peers))

    started = []

    def go(cp):
        cp.start()
        started.append(cp)

    def forward(stream, hop):
        if hop < 2:
            for way in (0, 1):
                go(z_copy(way, stream, hop + 1))
        else:
            go(far_copy(stream))

    def arrive_z(stream, hop):
        kind, far = STREAM[stream]
        for way in (0, 1):
            z_copy(way, stream, hop).wait_recv()
        if kind == GATE:
            forward(stream, hop)
        for off in (-(hop + 1), hop + 1):
            if kind == GATE:
                go(y_copy(GATE, off))
            go(c_copy(kind, far, off))

    def arrive_far(stream):
        kind, far = STREAM[stream]
        far_copy(stream).wait_recv()
        if kind == GATE:
            go(y_copy(GATE, 4))
        go(c_copy(kind, far, 4))

    def arrive_y(off):
        y_copy(GATE, off).wait_recv()
        go(c_copy(GATE, 1, off))

    def from_sibling(kind, far, off):
        c_copy(kind, far, off).wait_recv()

    def wgrad(kind, off):
        g = group(off)
        acc = (gate_acc, up_acc)[kind]
        for half in (0, 1):
            cols = pl.ds(half * 896, 896)
            prod = jnp.dot(xt[g], grads[kind, g, :, cols], preferred_element_type=jnp.float32)
            if off != 0:
                prod = acc[:, cols] + prod
            if off == 4:
                prod = prod * SCALE
            acc[:, cols] = prod

    def igrad(off):
        g = group(off)
        part[g] = jnp.dot(grads[GATE, g], wt[GATE], preferred_element_type=jnp.float32)

    def piece(step):
        return pl.ds(pl.multiple_of(((x + step) % NX) * PIECE, PIECE), PIECE)

    def g_copy(off, step):
        i = off % NZ
        return remote(
            part_b.at[group(off), :, piece(step), :], rx.at[i, step - 1],
            g_s.at[i, step - 1], g_r.at[i, step - 1], at_x(step),
        )

    def finish(off):
        g = group(off)
        prod = jnp.dot(grads[UP, g], wt[UP], preferred_element_type=jnp.float32)
        prod = (part[g] + prod).astype(jnp.bfloat16)
        for h in (0, 1):
            part_b[g, h] = prod[h * 128 : (h + 1) * 128]
        for step in (1, 2, 3):
            go(g_copy(off, step))

    def h_copy(off, h):
        return remote(
            sums.at[off % NZ, h], fin.at[tensor, h], h_s.at[off % NZ, h], h_r.at[tensor, h],
            {"dp": dp, "tensor": group(off)},
        )

    def to_owner(off, h, total):
        sums[off % NZ, h] = total.astype(jnp.bfloat16)
        pl.when(tensor != group(off))(lambda: h_copy(off, h).start())

        @pl.when(tensor == group(off))
        def _():
            fin[tensor, h] = total.astype(jnp.bfloat16)

    def collect(off):
        total = part_b[group(off), :, piece(0), :].astype(jnp.float32)
        for step in (1, 2, 3):
            g_copy(off, step).wait_recv()
            total = total + rx[off % NZ, step - 1].astype(jnp.float32)
        for h in (0, 1):
            to_owner(off, h, total[h])

    def last_half(far):
        return 1 - yh if far else yh

    def last_copy(far, step):
        h = last_half(far)
        return remote(
            part_b.at[group(4), h, piece(step), :], rx.at[4, step - 1, h],
            g_s.at[4 + 4 * far, step - 1], g_r.at[4 + 4 * far, step - 1], at_x(step),
        )

    def last_finish(far):
        g, h = group(4), last_half(far)
        rows = pl.ds(pl.multiple_of(h * 128, 128), 128)
        prod = jnp.dot(grads[UP, g, rows, :], wt[UP], preferred_element_type=jnp.float32)
        part_b[g, h] = (part[g, rows, :] + prod).astype(jnp.bfloat16)
        for step in (1, 2, 3):
            go(last_copy(far, step))

    def collect_last(far):
        h = last_half(far)
        total = part_b[group(4), h, piece(0), :].astype(jnp.float32)
        for step in (1, 2, 3):
            last_copy(far, step).wait_recv()
            total = total + rx[4, step - 1, h].astype(jnp.float32)
        to_owner(4, h, total)

    for way in (0, 1):
        go(z_copy(way, 0, 0))
    go(y_copy(UP, 0))
    for way in (0, 1):
        go(z_copy(way, 1, 0))
    go(c_copy(UP, 0, 0))
    go(c_copy(GATE, 0, 0))
    go(x_copy(0))
    go(y_copy(GATE, 0))
    for slot in (1, 2, 3):
        go(x_copy(slot))

    for cp in w_loads:
        cp.wait()

    def flip_w(i, _):
        cols = pl.ds(pl.multiple_of(i * 256, 256), 256)
        for kind in (GATE, UP):
            wt[kind, cols, :] = w[kind, :, cols].T
        return 0

    lax.fori_loop(0, HID // 256, flip_w, 0)

    arrive_z(0, 0)
    y_copy(UP, 0).wait_recv()
    for way in (0, 1):
        go(z_copy(way, 2, 0))
    go(c_copy(UP, 1, 0))
    x_copy(0).wait_recv()
    for slot in (4, 5, 6):
        go(x_copy(slot))
    arrive_z(1, 0)

    x_load.wait()
    for slot in range(1, 7):
        x_copy(slot).wait_recv()

    def flip_x(i, _):
        xt[i] = xs[i].T
        return 0

    lax.fori_loop(0, NZ, flip_x, 0)

    def from_both(kind, off):
        for far in (0, 1):
            from_sibling(kind, far, off)

    def do(kind, off):
        from_both(kind, off)
        if kind == GATE:
            igrad(off)
        else:
            finish(off)
        wgrad(kind, off)

    arrive_y(0)
    arrive_z(0, 1)
    forward(1, 0)
    do(GATE, 0)
    do(UP, 0)
    arrive_y(-1)
    arrive_z(2, 0)
    do(GATE, -1)
    do(UP, -1)
    arrive_y(1)
    arrive_z(0, 2)
    forward(2, 0)
    do(GATE, 1)
    do(UP, 1)
    arrive_y(-2)
    arrive_z(1, 1)
    forward(1, 1)
    collect(0)
    do(GATE, -2)
    arrive_far(0)
    arrive_y(2)
    collect(-1)
    collect(1)
    do(GATE, 2)
    arrive_z(2, 1)
    forward(2, 1)
    arrive_y(-3)
    do(UP, -2)
    do(GATE, -3)
    arrive_z(1, 2)
    forward(1, 2)
    do(UP, 2)
    arrive_y(3)
    do(GATE, 3)
    arrive_z(2, 2)
    forward(2, 2)
    arrive_y(4)
    collect(-2)
    collect(2)
    from_both(UP, -3)
    finish(-3)
    from_both(UP, 3)
    finish(3)
    arrive_far(1)
    from_both(GATE, 4)
    igrad(4)
    wgrad(UP, -3)
    from_sibling(UP, 0, 4)
    last_finish(0)
    arrive_far(2)
    wgrad(UP, 3)
    from_sibling(UP, 1, 4)
    last_finish(1)
    collect(-3)
    collect(3)
    wgrad(GATE, 4)
    collect_last(0)
    collect_last(1)
    wgrad(UP, 4)

    def arrived(i, _):
        @pl.when(i != tensor)
        def _():
            for h in (0, 1):
                remote(fin.at[i, h], fin.at[i, h], h_s.at[0, h], h_r.at[i, h], sibling).wait_recv()

        return 0

    lax.fori_loop(0, NZ, arrived, 0)
    for i in range(NX):
        total = fin[2 * i].astype(jnp.float32) + fin[2 * i + 1].astype(jnp.float32)
        for h in (0, 1):
            igrad_out[h * 128 + i * PIECE : h * 128 + (i + 1) * PIECE, :] = total[h].astype(jnp.bfloat16)

    for cp in started:
        cp.wait_send()
    for off in OFFS:
        @pl.when(tensor != group(off))
        def _():
            for h in (0, 1):
                h_copy(off, h).wait_send()


def write_out(*refs):
    n = len(refs) // 2
    sem = refs[-1]
    copies = []
    for i in range(n):
        rows = refs[i].shape[0] // PARTS
        for j in range(PARTS):
            at = pl.ds(j * rows, rows)
            copies.append(pltpu.make_async_copy(refs[i].at[at, :], refs[n + i].at[at, :], sem.at[i, j]))
    for cp in copies:
        cp.start()
    for cp in copies:
        cp.wait()


def per_device(*args):
    bf16, f32 = jnp.bfloat16, jnp.float32
    dma = pltpu.SemaphoreType.DMA
    hbm = pl.BlockSpec(memory_space=pl.ANY)
    vmem = pl.BlockSpec(memory_space=pltpu.VMEM)
    outs = (((GROUP, FEAT), bf16), ((FEAT, HID), f32), ((FEAT, HID), f32))
    held = pl.pallas_call(
        kernel,
        out_shape=tuple(pltpu.VMEM(*o) for o in outs),
        in_specs=[hbm] * 6,
        out_specs=(vmem,) * 3,
        scratch_shapes=[
            pltpu.VMEM((2, NZ, GROUP, HID), bf16),
            pltpu.VMEM((NZ, GROUP, FEAT), bf16),
            pltpu.VMEM((NZ, FEAT, GROUP), bf16),
            pltpu.VMEM((2, FEAT, HID), bf16),
            pltpu.VMEM((2, HID, FEAT), bf16),
            pltpu.VMEM((NZ, GROUP, FEAT), f32),
            pltpu.VMEM((NZ, 2, 128, FEAT), bf16),
            pltpu.VMEM((NZ, 3, 2, PIECE, FEAT), bf16),
            pltpu.VMEM((NZ, 2, PIECE, FEAT), bf16),
            pltpu.VMEM((NZ, 2, PIECE, FEAT), bf16),
            pltpu.VMEM((3, ROWS, HID), bf16),
            dma((6,)),
            dma((2, 3, 3)), dma((2, 3, 3)),
            dma((3,)), dma((3,)),
            dma((NZ + 1,)), dma((NZ + 1,)),
            dma((2, 2, NZ)), dma((2, 2, NZ)),
            dma((7,)), dma((7,)),
            dma((NZ + 1, 3)), dma((NZ + 1, 3)),
            dma((NZ, 2)), dma((NZ, 2)),
        ],
        compiler_params=pltpu.CompilerParams(
            collective_id=0, has_side_effects=True, vmem_limit_bytes=VMEM_BYTES
        ),
        cost_estimate=pl.CostEstimate(flops=7516192768, bytes_accessed=8 * 2**20, transcendentals=0),
        name="swiglu_bwd",
    )(*args)
    return tuple(
        pl.pallas_call(
            write_out,
            out_shape=tuple(jax.ShapeDtypeStruct(*o) for o in outs),
            in_specs=[hbm] * 3,
            out_specs=(hbm,) * 3,
            scratch_shapes=[dma((3, PARTS))],
            compiler_params=pltpu.CompilerParams(vmem_limit_bytes=4 * 2**20),
            name="write_out",
        )(*held)
    )


def solution(mesh):
    in_specs = (
        P("tensor", "dp"),
        P("dp", "tensor"),
        P("dp", "tensor"),
        P("dp", "tensor"),
        P("dp", "tensor"),
        P("dp", "tensor"),
    )
    out_specs = (P("tensor", "dp"), P("dp", "tensor"), P("dp", "tensor"))
    return jax.shard_map(
        per_device, mesh=mesh, in_specs=in_specs, out_specs=out_specs, check_vma=False
    )
```

```python
import functools
import math

import jax
import jax.numpy as jnp
from jax import lax
from jax.experimental import pallas as pl
from jax.experimental.pallas import tpu as pltpu
from jax.sharding import PartitionSpec as P

MESH = pl.DeviceIdType.MESH
ROWS = 64
GROUP = 256
HID = 1792
FEAT = 256
NZ = 8
NX = 4
PIECE = 128 // NX
PARTS = 1
GATE, UP = 0, 1
VMEM_BYTES = 56 * 2**20
SCALE = 1.0 / math.sqrt(2048)
OFFS = (0, -1, 1, -2, 2, -3, 3, 4)


def kernel(
    inputs, gate_pre, up_pre, hidden_grad, gate_weight, up_weight,
    igrad_out, gate_acc, up_acc,
    grads, xs, xt, w, wt, part, part_b, rx, sums, fin, pre,
    loc, z_s, z_r, f_s, f_r, y_s, y_r, c_s, c_r, x_s, x_r, g_s, g_r, h_s, h_r,
):
    dp, tensor = lax.axis_index("dp"), lax.axis_index("tensor")
    z, yh, c = dp // 4, (dp // 2) % 2, dp % 2
    x, yl = tensor // 2, tensor % 2

    def at_z(step):
        return {"dp": ((z + step + NZ) % NZ) * 4 + yh * 2 + c, "tensor": tensor}

    opposite = {"dp": z * 4 + (1 - yh) * 2 + c, "tensor": tensor}
    sibling = {"dp": z * 4 + yh * 2 + (1 - c), "tensor": tensor}
    partner = {"dp": dp, "tensor": x * 2 + (1 - yl)}

    def at_x(step):
        return {"dp": dp, "tensor": ((x + step) % NX) * 2 + yl}

    def group(off):
        return (z + off + NZ) % NZ

    own_rows = pl.multiple_of(yh * 128 + c * ROWS, ROWS)
    opp_rows = pl.multiple_of((1 - yh) * 128 + c * ROWS, ROWS)

    def block(kind, src_z, far):
        return grads.at[kind, src_z, pl.ds(opp_rows if far else own_rows, ROWS), :]

    def remote(src, dst, s, r, dev):
        return pltpu.make_async_remote_copy(
            src_ref=src, dst_ref=dst, send_sem=s, recv_sem=r, device_id=dev, device_id_type=MESH
        )

    STREAM = ((GATE, 0), (UP, 0), (UP, 1))

    def z_copy(way, stream, hop):
        kind, far = STREAM[stream]
        step = 1 - 2 * way
        b = block(kind, group(-step * hop), far)
        return remote(b, b, z_s.at[way, stream, hop], z_r.at[way, stream, hop], at_z(step))

    def far_copy(stream):
        kind, far = STREAM[stream]
        step = 1 - 2 * c
        b = block(kind, group(-3 * step), far)
        return remote(b, b, f_s.at[stream], f_r.at[stream], at_z(step))

    def y_copy(kind, off):
        slot = NZ if kind == UP else off % NZ
        b = block(kind, group(off), 0)
        return remote(b, b, y_s.at[slot], y_r.at[slot], opposite)

    def c_copy(kind, far, off):
        b = block(kind, group(off), far)
        i = off % NZ
        return remote(b, b, c_s.at[kind, far, i], c_r.at[kind, far, i], sibling)

    def x_copy(slot):
        if slot == 0:
            return remote(inputs, xs.at[tensor], x_s.at[0], x_r.at[0], partner)
        if slot <= 3:
            return remote(inputs, xs.at[tensor], x_s.at[slot], x_r.at[slot], at_x(slot))
        b = xs.at[x * 2 + (1 - yl)]
        return remote(b, b, x_s.at[slot], x_r.at[slot], at_x(slot - 3))

    pre_loads = [
        pltpu.make_async_copy(ref, pre.at[i], loc.at[i])
        for i, ref in enumerate((gate_pre, up_pre, hidden_grad))
    ]
    w_loads = [
        pltpu.make_async_copy(ref, w.at[i], loc.at[3 + i])
        for i, ref in enumerate((gate_weight, up_weight))
    ]
    x_load = pltpu.make_async_copy(inputs, xs.at[tensor], loc.at[5])
    for cp in pre_loads + w_loads + [x_load]:
        cp.start()

    barrier = pltpu.get_barrier_semaphore()
    peers = [at_z(1), at_z(-1), opposite, sibling]
    peers += [{"dp": dp, "tensor": (tensor + i) % NZ} for i in range(1, NZ)]
    for peer in peers:
        pl.semaphore_signal(barrier, inc=1, device_id=peer, device_id_type=MESH)

    for cp in pre_loads:
        cp.wait()

    def elementwise(i, _):
        cols = pl.ds(pl.multiple_of(i * 256, 256), 256)
        gate_value = pre[0, :, cols].astype(jnp.float32)
        up_value = pre[1, :, cols].astype(jnp.float32)
        grad_value = pre[2, :, cols].astype(jnp.float32)
        sig = 1.0 / (1.0 + jnp.exp(-gate_value))
        grads[UP, z, pl.ds(own_rows, ROWS), cols] = (grad_value * gate_value * sig).astype(jnp.bfloat16)
        grads[GATE, z, pl.ds(own_rows, ROWS), cols] = (
            grad_value * up_value * sig * (1.0 + gate_value * (1.0 - sig))
        ).astype(jnp.bfloat16)
        return 0

    lax.fori_loop(0, HID // 256, elementwise, 0)
    pl.semaphore_wait(barrier, len(peers))

    started = []

    def go(cp):
        cp.start()
        started.append(cp)

    def forward(stream, hop):
        if hop < 2:
            for way in (0, 1):
                go(z_copy(way, stream, hop + 1))
        else:
            go(far_copy(stream))

    def arrive_z(stream, hop):
        kind, far = STREAM[stream]
        for way in (0, 1):
            z_copy(way, stream, hop).wait_recv()
        if kind == GATE:
            forward(stream, hop)
        for off in (-(hop + 1), hop + 1):
            if kind == GATE:
                go(y_copy(GATE, off))
            go(c_copy(kind, far, off))

    def arrive_far(stream):
        kind, far = STREAM[stream]
        far_copy(stream).wait_recv()
        if kind == GATE:
            go(y_copy(GATE, 4))
        go(c_copy(kind, far, 4))

    def arrive_y(off):
        y_copy(GATE, off).wait_recv()
        go(c_copy(GATE, 1, off))

    def from_sibling(kind, far, off):
        c_copy(kind, far, off).wait_recv()

    def wgrad(kind, off):
        g = group(off)
        acc = (gate_acc, up_acc)[kind]
        for half in (0, 1):
            cols = pl.ds(half * 896, 896)
            prod = jnp.dot(xt[g], grads[kind, g, :, cols], preferred_element_type=jnp.float32)
            if off != 0:
                prod = acc[:, cols] + prod
            if off == 4:
                prod = prod * SCALE
            acc[:, cols] = prod

    def igrad(off):
        g = group(off)
        part[g] = jnp.dot(grads[GATE, g], wt[GATE], preferred_element_type=jnp.float32)

    def piece(step):
        return pl.ds(pl.multiple_of(((x + step) % NX) * PIECE, PIECE), PIECE)

    def g_copy(off, step):
        i = off % NZ
        return remote(
            part_b.at[group(off), :, piece(step), :], rx.at[i, step - 1],
            g_s.at[i, step - 1], g_r.at[i, step - 1], at_x(step),
        )

    def finish(off):
        g = group(off)
        prod = jnp.dot(grads[UP, g], wt[UP], preferred_element_type=jnp.float32)
        prod = (part[g] + prod).astype(jnp.bfloat16)
        for h in (0, 1):
            part_b[g, h] = prod[h * 128 : (h + 1) * 128]
        for step in (1, 2, 3):
            go(g_copy(off, step))

    def h_copy(off, h):
        return remote(
            sums.at[off % NZ, h], fin.at[tensor, h], h_s.at[off % NZ, h], h_r.at[tensor, h],
            {"dp": dp, "tensor": group(off)},
        )

    def to_owner(off, h, total):
        sums[off % NZ, h] = total.astype(jnp.bfloat16)
        pl.when(tensor != group(off))(lambda: h_copy(off, h).start())

        @pl.when(tensor == group(off))
        def _():
            fin[tensor, h] = total.astype(jnp.bfloat16)

    def collect(off):
        total = part_b[group(off), :, piece(0), :].astype(jnp.float32)
        for step in (1, 2, 3):
            g_copy(off, step).wait_recv()
            total = total + rx[off % NZ, step - 1].astype(jnp.float32)
        for h in (0, 1):
            to_owner(off, h, total[h])

    def last_half(far):
        return 1 - yh if far else yh

    def last_copy(far, step):
        h = last_half(far)
        return remote(
            part_b.at[group(4), h, piece(step), :], rx.at[4, step - 1, h],
            g_s.at[4 + 4 * far, step - 1], g_r.at[4 + 4 * far, step - 1], at_x(step),
        )

    def last_finish(far):
        g, h = group(4), last_half(far)
        rows = pl.ds(pl.multiple_of(h * 128, 128), 128)
        prod = jnp.dot(grads[UP, g, rows, :], wt[UP], preferred_element_type=jnp.float32)
        part_b[g, h] = (part[g, rows, :] + prod).astype(jnp.bfloat16)
        for step in (1, 2, 3):
            go(last_copy(far, step))

    def collect_last(far):
        h = last_half(far)
        total = part_b[group(4), h, piece(0), :].astype(jnp.float32)
        for step in (1, 2, 3):
            last_copy(far, step).wait_recv()
            total = total + rx[4, step - 1, h].astype(jnp.float32)
        to_owner(4, h, total)

    for way in (0, 1):
        go(z_copy(way, 0, 0))
    go(y_copy(UP, 0))
    for way in (0, 1):
        go(z_copy(way, 1, 0))
    go(c_copy(UP, 0, 0))
    go(c_copy(GATE, 0, 0))
    go(x_copy(0))
    go(y_copy(GATE, 0))
    for slot in (1, 2, 3):
        go(x_copy(slot))

    for cp in w_loads:
        cp.wait()

    def flip_w(i, _):
        cols = pl.ds(pl.multiple_of(i * 256, 256), 256)
        for kind in (GATE, UP):
            wt[kind, cols, :] = w[kind, :, cols].T
        return 0

    lax.fori_loop(0, HID // 256, flip_w, 0)

    arrive_z(0, 0)
    y_copy(UP, 0).wait_recv()
    for way in (0, 1):
        go(z_copy(way, 2, 0))
    go(c_copy(UP, 1, 0))
    x_copy(0).wait_recv()
    for slot in (4, 5, 6):
        go(x_copy(slot))
    arrive_z(1, 0)

    x_load.wait()
    for slot in range(1, 7):
        x_copy(slot).wait_recv()

    def flip_x(i, _):
        xt[i] = xs[i].T
        return 0

    lax.fori_loop(0, NZ, flip_x, 0)

    def from_both(kind, off):
        for far in (0, 1):
            from_sibling(kind, far, off)

    def do(kind, off):
        from_both(kind, off)
        if kind == GATE:
            igrad(off)
        else:
            finish(off)
        wgrad(kind, off)

    arrive_y(0)
    arrive_z(0, 1)
    forward(1, 0)
    do(GATE, 0)
    do(UP, 0)
    arrive_y(-1)
    arrive_z(2, 0)
    do(GATE, -1)
    do(UP, -1)
    arrive_y(1)
    arrive_z(0, 2)
    forward(2, 0)
    do(GATE, 1)
    do(UP, 1)
    arrive_y(-2)
    arrive_z(1, 1)
    forward(1, 1)
    collect(0)
    do(GATE, -2)
    arrive_far(0)
    arrive_y(2)
    collect(-1)
    collect(1)
    arrive_z(2, 1)
    forward(2, 1)
    do(GATE, 2)
    arrive_y(-3)
    do(UP, -2)
    do(GATE, -3)
    arrive_z(1, 2)
    forward(1, 2)
    do(UP, 2)
    arrive_y(3)
    arrive_z(2, 2)
    forward(2, 2)
    do(GATE, 3)
    from_both(UP, -3)
    finish(-3)
    arrive_y(4)
    arrive_far(1)
    from_both(UP, 3)
    finish(3)
    collect(-2)
    collect(2)
    from_both(GATE, 4)
    igrad(4)
    from_sibling(UP, 0, 4)
    last_finish(0)
    arrive_far(2)
    wgrad(UP, -3)
    from_sibling(UP, 1, 4)
    last_finish(1)
    collect(-3)
    collect(3)
    wgrad(UP, 3)
    collect_last(0)
    wgrad(GATE, 4)
    for cp in started:
        cp.wait_send()
    collect_last(1)
    wgrad(UP, 4)

    def arrived(i, _):
        @pl.when(i != tensor)
        def _():
            for h in (0, 1):
                remote(fin.at[i, h], fin.at[i, h], h_s.at[0, h], h_r.at[i, h], sibling).wait_recv()

        return 0

    lax.fori_loop(0, NZ, arrived, 0)
    for i in range(NX):
        total = fin[2 * i].astype(jnp.float32) + fin[2 * i + 1].astype(jnp.float32)
        for h in (0, 1):
            igrad_out[h * 128 + i * PIECE : h * 128 + (i + 1) * PIECE, :] = total[h].astype(jnp.bfloat16)

    for off in OFFS:
        @pl.when(tensor != group(off))
        def _():
            for h in (0, 1):
                h_copy(off, h).wait_send()


def write_out(*refs):
    n = len(refs) // 2
    sem = refs[-1]
    copies = []
    for i in range(n):
        rows = refs[i].shape[0] // PARTS
        for j in range(PARTS):
            at = pl.ds(j * rows, rows)
            copies.append(pltpu.make_async_copy(refs[i].at[at, :], refs[n + i].at[at, :], sem.at[i, j]))
    for cp in copies:
        cp.start()
    for cp in copies:
        cp.wait()


def per_device(*args):
    bf16, f32 = jnp.bfloat16, jnp.float32
    dma = pltpu.SemaphoreType.DMA
    hbm = pl.BlockSpec(memory_space=pl.ANY)
    vmem = pl.BlockSpec(memory_space=pltpu.VMEM)
    outs = (((GROUP, FEAT), bf16), ((FEAT, HID), f32), ((FEAT, HID), f32))
    held = pl.pallas_call(
        kernel,
        out_shape=tuple(pltpu.VMEM(*o) for o in outs),
        in_specs=[hbm] * 6,
        out_specs=(vmem,) * 3,
        scratch_shapes=[
            pltpu.VMEM((2, NZ, GROUP, HID), bf16),
            pltpu.VMEM((NZ, GROUP, FEAT), bf16),
            pltpu.VMEM((NZ, FEAT, GROUP), bf16),
            pltpu.VMEM((2, FEAT, HID), bf16),
            pltpu.VMEM((2, HID, FEAT), bf16),
            pltpu.VMEM((NZ, GROUP, FEAT), f32),
            pltpu.VMEM((NZ, 2, 128, FEAT), bf16),
            pltpu.VMEM((NZ, 3, 2, PIECE, FEAT), bf16),
            pltpu.VMEM((NZ, 2, PIECE, FEAT), bf16),
            pltpu.VMEM((NZ, 2, PIECE, FEAT), bf16),
            pltpu.VMEM((3, ROWS, HID), bf16),
            dma((6,)),
            dma((2, 3, 3)), dma((2, 3, 3)),
            dma((3,)), dma((3,)),
            dma((NZ + 1,)), dma((NZ + 1,)),
            dma((2, 2, NZ)), dma((2, 2, NZ)),
            dma((7,)), dma((7,)),
            dma((NZ + 1, 3)), dma((NZ + 1, 3)),
            dma((NZ, 2)), dma((NZ, 2)),
        ],
        compiler_params=pltpu.CompilerParams(
            collective_id=0, has_side_effects=True, vmem_limit_bytes=VMEM_BYTES
        ),
        cost_estimate=pl.CostEstimate(flops=7516192768, bytes_accessed=8 * 2**20, transcendentals=0),
        name="swiglu_bwd",
    )(*args)
    return tuple(
        pl.pallas_call(
            write_out,
            out_shape=tuple(jax.ShapeDtypeStruct(*o) for o in outs),
            in_specs=[hbm] * 3,
            out_specs=(hbm,) * 3,
            scratch_shapes=[dma((3, PARTS))],
            compiler_params=pltpu.CompilerParams(vmem_limit_bytes=4 * 2**20),
            name="write_out",
        )(*held)
    )


def solution(mesh):
    in_specs = (
        P("tensor", "dp"),
        P("dp", "tensor"),
        P("dp", "tensor"),
        P("dp", "tensor"),
        P("dp", "tensor"),
        P("dp", "tensor"),
    )
    out_specs = (P("tensor", "dp"), P("dp", "tensor"), P("dp", "tensor"))
    return jax.shard_map(
        per_device, mesh=mesh, in_specs=in_specs, out_specs=out_specs, check_vma=False
    )
```

```python
import functools
import math

import jax
import jax.numpy as jnp
from jax import lax
from jax.experimental import pallas as pl
from jax.experimental.pallas import tpu as pltpu
from jax.sharding import PartitionSpec as P

MESH = pl.DeviceIdType.MESH
ROWS = 64
GROUP = 256
HID = 1792
FEAT = 256
NZ = 8
NX = 4
PIECE = 128 // NX
PARTS = 1
GATE, UP = 0, 1
VMEM_BYTES = 56 * 2**20
SCALE = 1.0 / math.sqrt(2048)
OFFS = (0, -1, 1, -2, 2, -3, 3, 4)


def kernel(
    inputs, gate_pre, up_pre, hidden_grad, gate_weight, up_weight,
    igrad_out, gate_acc, up_acc,
    grads, xs, xt, w, wt, part, part_b, rx, sums, fin, pre,
    loc, z_s, z_r, f_s, f_r, y_s, y_r, c_s, c_r, x_s, x_r, g_s, g_r, h_s, h_r,
):
    dp, tensor = lax.axis_index("dp"), lax.axis_index("tensor")
    z, yh, c = dp // 4, (dp // 2) % 2, dp % 2
    x, yl = tensor // 2, tensor % 2

    def at_z(step):
        return {"dp": ((z + step + NZ) % NZ) * 4 + yh * 2 + c, "tensor": tensor}

    opposite = {"dp": z * 4 + (1 - yh) * 2 + c, "tensor": tensor}
    sibling = {"dp": z * 4 + yh * 2 + (1 - c), "tensor": tensor}
    partner = {"dp": dp, "tensor": x * 2 + (1 - yl)}

    def at_x(step):
        return {"dp": dp, "tensor": ((x + step) % NX) * 2 + yl}

    def group(off):
        return (z + off + NZ) % NZ

    own_rows = pl.multiple_of(yh * 128 + c * ROWS, ROWS)
    opp_rows = pl.multiple_of((1 - yh) * 128 + c * ROWS, ROWS)

    def block(kind, src_z, far):
        return grads.at[kind, src_z, pl.ds(opp_rows if far else own_rows, ROWS), :]

    def remote(src, dst, s, r, dev):
        return pltpu.make_async_remote_copy(
            src_ref=src, dst_ref=dst, send_sem=s, recv_sem=r, device_id=dev, device_id_type=MESH
        )

    STREAM = ((GATE, 0), (UP, 0), (UP, 1))

    def z_copy(way, stream, hop):
        kind, far = STREAM[stream]
        step = 1 - 2 * way
        b = block(kind, group(-step * hop), far)
        return remote(b, b, z_s.at[way, stream, hop], z_r.at[way, stream, hop], at_z(step))

    def far_copy(stream):
        kind, far = STREAM[stream]
        step = 1 - 2 * c
        b = block(kind, group(-3 * step), far)
        return remote(b, b, f_s.at[stream], f_r.at[stream], at_z(step))

    def y_copy(kind, off):
        slot = NZ if kind == UP else off % NZ
        b = block(kind, group(off), 0)
        return remote(b, b, y_s.at[slot], y_r.at[slot], opposite)

    def c_copy(kind, far, off):
        b = block(kind, group(off), far)
        i = off % NZ
        return remote(b, b, c_s.at[kind, far, i], c_r.at[kind, far, i], sibling)

    def x_copy(slot):
        if slot == 0:
            return remote(inputs, xs.at[tensor], x_s.at[0], x_r.at[0], partner)
        if slot <= 3:
            return remote(inputs, xs.at[tensor], x_s.at[slot], x_r.at[slot], at_x(slot))
        b = xs.at[x * 2 + (1 - yl)]
        return remote(b, b, x_s.at[slot], x_r.at[slot], at_x(slot - 3))

    pre_loads = [
        pltpu.make_async_copy(ref, pre.at[i], loc.at[i])
        for i, ref in enumerate((gate_pre, up_pre, hidden_grad))
    ]
    w_loads = [
        pltpu.make_async_copy(ref, w.at[i], loc.at[3 + i])
        for i, ref in enumerate((gate_weight, up_weight))
    ]
    x_load = pltpu.make_async_copy(inputs, xs.at[tensor], loc.at[5])
    for cp in pre_loads + w_loads + [x_load]:
        cp.start()

    barrier = pltpu.get_barrier_semaphore()
    peers = [at_z(1), at_z(-1), opposite, sibling]
    peers += [{"dp": dp, "tensor": (tensor + i) % NZ} for i in range(1, NZ)]
    for peer in peers:
        pl.semaphore_signal(barrier, inc=1, device_id=peer, device_id_type=MESH)

    for cp in pre_loads:
        cp.wait()

    def elementwise(i, _):
        cols = pl.ds(pl.multiple_of(i * 256, 256), 256)
        gate_value = pre[0, :, cols].astype(jnp.float32)
        up_value = pre[1, :, cols].astype(jnp.float32)
        grad_value = pre[2, :, cols].astype(jnp.float32)
        sig = 1.0 / (1.0 + jnp.exp(-gate_value))
        grads[UP, z, pl.ds(own_rows, ROWS), cols] = (grad_value * gate_value * sig).astype(jnp.bfloat16)
        grads[GATE, z, pl.ds(own_rows, ROWS), cols] = (
            grad_value * up_value * sig * (1.0 + gate_value * (1.0 - sig))
        ).astype(jnp.bfloat16)
        return 0

    lax.fori_loop(0, HID // 256, elementwise, 0)
    pl.semaphore_wait(barrier, len(peers))

    started = []

    def go(cp):
        cp.start()
        started.append(cp)

    def forward(stream, hop):
        if hop < 2:
            for way in (0, 1):
                go(z_copy(way, stream, hop + 1))
        else:
            go(far_copy(stream))

    def arrive_z(stream, hop):
        kind, far = STREAM[stream]
        for way in (0, 1):
            z_copy(way, stream, hop).wait_recv()
        if kind == GATE:
            forward(stream, hop)
        for off in (-(hop + 1), hop + 1):
            if kind == GATE:
                go(y_copy(GATE, off))
            go(c_copy(kind, far, off))

    def arrive_far(stream):
        kind, far = STREAM[stream]
        far_copy(stream).wait_recv()
        if kind == GATE:
            go(y_copy(GATE, 4))
        go(c_copy(kind, far, 4))

    def arrive_y(off):
        y_copy(GATE, off).wait_recv()
        go(c_copy(GATE, 1, off))

    def from_sibling(kind, far, off):
        c_copy(kind, far, off).wait_recv()

    def wgrad(kind, off):
        g = group(off)
        acc = (gate_acc, up_acc)[kind]
        for half in (0, 1):
            cols = pl.ds(half * 896, 896)
            prod = jnp.dot(xt[g], grads[kind, g, :, cols], preferred_element_type=jnp.float32)
            if off != 0:
                prod = acc[:, cols] + prod
            if off == 4:
                prod = prod * SCALE
            acc[:, cols] = prod

    def igrad(off):
        g = group(off)
        part[g] = jnp.dot(grads[GATE, g], wt[GATE], preferred_element_type=jnp.float32)

    def piece(step):
        return pl.ds(pl.multiple_of(((x + step) % NX) * PIECE, PIECE), PIECE)

    def g_copy(off, step):
        i = off % NZ
        return remote(
            part_b.at[group(off), :, piece(step), :], rx.at[i, step - 1],
            g_s.at[i, step - 1], g_r.at[i, step - 1], at_x(step),
        )

    def finish(off):
        g = group(off)
        prod = jnp.dot(grads[UP, g], wt[UP], preferred_element_type=jnp.float32)
        prod = (part[g] + prod).astype(jnp.bfloat16)
        for h in (0, 1):
            part_b[g, h] = prod[h * 128 : (h + 1) * 128]
        for step in (1, 2, 3):
            go(g_copy(off, step))

    def h_copy(off, h):
        return remote(
            sums.at[off % NZ, h], fin.at[tensor, h], h_s.at[off % NZ, h], h_r.at[tensor, h],
            {"dp": dp, "tensor": group(off)},
        )

    def to_owner(off, h, total):
        sums[off % NZ, h] = total.astype(jnp.bfloat16)
        pl.when(tensor != group(off))(lambda: h_copy(off, h).start())

        @pl.when(tensor == group(off))
        def _():
            fin[tensor, h] = total.astype(jnp.bfloat16)

    def collect(off):
        total = part_b[group(off), :, piece(0), :].astype(jnp.float32)
        for step in (1, 2, 3):
            g_copy(off, step).wait_recv()
            total = total + rx[off % NZ, step - 1].astype(jnp.float32)
        for h in (0, 1):
            to_owner(off, h, total[h])

    def last_half(far):
        return 1 - yh if far else yh

    def last_copy(far, step):
        h = last_half(far)
        return remote(
            part_b.at[group(4), h, piece(step), :], rx.at[4, step - 1, h],
            g_s.at[4 + 4 * far, step - 1], g_r.at[4 + 4 * far, step - 1], at_x(step),
        )

    def last_finish(far):
        g, h = group(4), last_half(far)
        rows = pl.ds(pl.multiple_of(h * 128, 128), 128)
        prod = jnp.dot(grads[UP, g, rows, :], wt[UP], preferred_element_type=jnp.float32)
        part_b[g, h] = (part[g, rows, :] + prod).astype(jnp.bfloat16)
        for step in (1, 2, 3):
            go(last_copy(far, step))

    def collect_last(far):
        h = last_half(far)
        total = part_b[group(4), h, piece(0), :].astype(jnp.float32)
        for step in (1, 2, 3):
            last_copy(far, step).wait_recv()
            total = total + rx[4, step - 1, h].astype(jnp.float32)
        to_owner(4, h, total)

    for way in (0, 1):
        go(z_copy(way, 0, 0))
    go(y_copy(UP, 0))
    for way in (0, 1):
        go(z_copy(way, 1, 0))
    go(c_copy(UP, 0, 0))
    go(c_copy(GATE, 0, 0))
    go(x_copy(0))
    go(y_copy(GATE, 0))
    for slot in (1, 2, 3):
        go(x_copy(slot))

    for cp in w_loads:
        cp.wait()

    def flip_w(i, _):
        cols = pl.ds(pl.multiple_of(i * 256, 256), 256)
        for kind in (GATE, UP):
            wt[kind, cols, :] = w[kind, :, cols].T
        return 0

    lax.fori_loop(0, HID // 256, flip_w, 0)

    arrive_z(0, 0)
    y_copy(UP, 0).wait_recv()
    for way in (0, 1):
        go(z_copy(way, 2, 0))
    go(c_copy(UP, 1, 0))
    x_copy(0).wait_recv()
    for slot in (4, 5, 6):
        go(x_copy(slot))
    arrive_z(1, 0)

    x_load.wait()
    for slot in range(1, 7):
        x_copy(slot).wait_recv()

    def flip_x(i, _):
        xt[i] = xs[i].T
        return 0

    lax.fori_loop(0, NZ, flip_x, 0)

    def from_both(kind, off):
        for far in (0, 1):
            from_sibling(kind, far, off)

    def do(kind, off):
        from_both(kind, off)
        if kind == GATE:
            igrad(off)
        else:
            finish(off)
        wgrad(kind, off)

    arrive_y(0)
    arrive_z(0, 1)
    forward(1, 0)
    do(GATE, 0)
    do(UP, 0)
    arrive_y(-1)
    arrive_z(2, 0)
    do(GATE, -1)
    do(UP, -1)
    arrive_y(1)
    arrive_z(0, 2)
    forward(2, 0)
    do(GATE, 1)
    do(UP, 1)
    arrive_y(-2)
    arrive_z(1, 1)
    forward(1, 1)
    collect(0)
    do(GATE, -2)
    arrive_far(0)
    arrive_y(2)
    collect(-1)
    collect(1)
    arrive_z(2, 1)
    forward(2, 1)
    do(GATE, 2)
    arrive_y(-3)
    do(UP, -2)
    do(GATE, -3)
    arrive_z(1, 2)
    forward(1, 2)
    do(UP, 2)
    arrive_y(3)
    arrive_z(2, 2)
    forward(2, 2)
    do(GATE, 3)
    from_both(UP, -3)
    finish(-3)
    arrive_y(4)
    arrive_far(1)
    from_both(UP, 3)
    finish(3)
    collect(-2)
    collect(2)
    from_both(GATE, 4)
    igrad(4)
    from_sibling(UP, 0, 4)
    last_finish(0)
    arrive_far(2)
    wgrad(UP, -3)
    from_sibling(UP, 1, 4)
    last_finish(1)
    collect(-3)
    collect(3)
    wgrad(UP, 3)
    collect_last(0)
    collect_last(1)
    wgrad(GATE, 4)
    wgrad(UP, 4)
    for cp in started:
        cp.wait_send()

    def arrived(i, _):
        @pl.when(i != tensor)
        def _():
            for h in (0, 1):
                remote(fin.at[i, h], fin.at[i, h], h_s.at[0, h], h_r.at[i, h], sibling).wait_recv()

        return 0

    lax.fori_loop(0, NZ, arrived, 0)
    for i in range(NX):
        total = fin[2 * i].astype(jnp.float32) + fin[2 * i + 1].astype(jnp.float32)
        for h in (0, 1):
            igrad_out[h * 128 + i * PIECE : h * 128 + (i + 1) * PIECE, :] = total[h].astype(jnp.bfloat16)

    for off in OFFS:
        @pl.when(tensor != group(off))
        def _():
            for h in (0, 1):
                h_copy(off, h).wait_send()


def write_out(*refs):
    n = len(refs) // 2
    sem = refs[-1]
    copies = []
    for i in range(n):
        rows = refs[i].shape[0] // PARTS
        for j in range(PARTS):
            at = pl.ds(j * rows, rows)
            copies.append(pltpu.make_async_copy(refs[i].at[at, :], refs[n + i].at[at, :], sem.at[i, j]))
    for cp in copies:
        cp.start()
    for cp in copies:
        cp.wait()


def per_device(*args):
    bf16, f32 = jnp.bfloat16, jnp.float32
    dma = pltpu.SemaphoreType.DMA
    hbm = pl.BlockSpec(memory_space=pl.ANY)
    vmem = pl.BlockSpec(memory_space=pltpu.VMEM)
    outs = (((GROUP, FEAT), bf16), ((FEAT, HID), f32), ((FEAT, HID), f32))
    held = pl.pallas_call(
        kernel,
        out_shape=tuple(pltpu.VMEM(*o) for o in outs),
        in_specs=[hbm] * 6,
        out_specs=(vmem,) * 3,
        scratch_shapes=[
            pltpu.VMEM((2, NZ, GROUP, HID), bf16),
            pltpu.VMEM((NZ, GROUP, FEAT), bf16),
            pltpu.VMEM((NZ, FEAT, GROUP), bf16),
            pltpu.VMEM((2, FEAT, HID), bf16),
            pltpu.VMEM((2, HID, FEAT), bf16),
            pltpu.VMEM((NZ, GROUP, FEAT), f32),
            pltpu.VMEM((NZ, 2, 128, FEAT), bf16),
            pltpu.VMEM((NZ, 3, 2, PIECE, FEAT), bf16),
            pltpu.VMEM((NZ, 2, PIECE, FEAT), bf16),
            pltpu.VMEM((NZ, 2, PIECE, FEAT), bf16),
            pltpu.VMEM((3, ROWS, HID), bf16),
            dma((6,)),
            dma((2, 3, 3)), dma((2, 3, 3)),
            dma((3,)), dma((3,)),
            dma((NZ + 1,)), dma((NZ + 1,)),
            dma((2, 2, NZ)), dma((2, 2, NZ)),
            dma((7,)), dma((7,)),
            dma((NZ + 1, 3)), dma((NZ + 1, 3)),
            dma((NZ, 2)), dma((NZ, 2)),
        ],
        compiler_params=pltpu.CompilerParams(
            collective_id=0, has_side_effects=True, vmem_limit_bytes=VMEM_BYTES
        ),
        cost_estimate=pl.CostEstimate(flops=7516192768, bytes_accessed=8 * 2**20, transcendentals=0),
        name="swiglu_bwd",
    )(*args)
    return tuple(
        pl.pallas_call(
            write_out,
            out_shape=tuple(jax.ShapeDtypeStruct(*o) for o in outs),
            in_specs=[hbm] * 3,
            out_specs=(hbm,) * 3,
            scratch_shapes=[dma((3, PARTS))],
            compiler_params=pltpu.CompilerParams(vmem_limit_bytes=4 * 2**20),
            name="write_out",
        )(*held)
    )


def solution(mesh):
    in_specs = (
        P("tensor", "dp"),
        P("dp", "tensor"),
        P("dp", "tensor"),
        P("dp", "tensor"),
        P("dp", "tensor"),
        P("dp", "tensor"),
    )
    out_specs = (P("tensor", "dp"), P("dp", "tensor"), P("dp", "tensor"))
    return jax.shard_map(
        per_device, mesh=mesh, in_specs=in_specs, out_specs=out_specs, check_vma=False
    )
```

```python
import functools
import math

import jax
import jax.numpy as jnp
from jax import lax
from jax.experimental import pallas as pl
from jax.experimental.pallas import tpu as pltpu
from jax.sharding import PartitionSpec as P

MESH = pl.DeviceIdType.MESH
ROWS = 64
GROUP = 256
HID = 1792
FEAT = 256
NZ = 8
NX = 4
PIECE = 128 // NX
PARTS = 1
GATE, UP = 0, 1
VMEM_BYTES = 56 * 2**20
SCALE = 1.0 / math.sqrt(2048)
OFFS = (0, -1, 1, -2, 2, -3, 3, 4)


def kernel(
    inputs, gate_pre, up_pre, hidden_grad, gate_weight, up_weight,
    igrad_out, gate_acc, up_acc,
    grads, xs, xt, w, wt, part, part_b, rx, sums, fin, pre,
    loc, z_s, z_r, f_s, f_r, y_s, y_r, c_s, c_r, x_s, x_r, g_s, g_r, h_s, h_r,
):
    dp, tensor = lax.axis_index("dp"), lax.axis_index("tensor")
    z, yh, c = dp // 4, (dp // 2) % 2, dp % 2
    x, yl = tensor // 2, tensor % 2

    def at_z(step):
        return {"dp": ((z + step + NZ) % NZ) * 4 + yh * 2 + c, "tensor": tensor}

    opposite = {"dp": z * 4 + (1 - yh) * 2 + c, "tensor": tensor}
    sibling = {"dp": z * 4 + yh * 2 + (1 - c), "tensor": tensor}
    partner = {"dp": dp, "tensor": x * 2 + (1 - yl)}

    def at_x(step):
        return {"dp": dp, "tensor": ((x + step) % NX) * 2 + yl}

    def group(off):
        return (z + off + NZ) % NZ

    own_rows = pl.multiple_of(yh * 128 + c * ROWS, ROWS)
    opp_rows = pl.multiple_of((1 - yh) * 128 + c * ROWS, ROWS)

    def block(kind, src_z, far):
        return grads.at[kind, src_z, pl.ds(opp_rows if far else own_rows, ROWS), :]

    def remote(src, dst, s, r, dev):
        return pltpu.make_async_remote_copy(
            src_ref=src, dst_ref=dst, send_sem=s, recv_sem=r, device_id=dev, device_id_type=MESH
        )

    STREAM = ((GATE, 0), (UP, 0), (UP, 1))

    def z_copy(way, stream, hop):
        kind, far = STREAM[stream]
        step = 1 - 2 * way
        b = block(kind, group(-step * hop), far)
        return remote(b, b, z_s.at[way, stream, hop], z_r.at[way, stream, hop], at_z(step))

    def far_copy(stream):
        kind, far = STREAM[stream]
        step = 1 - 2 * c
        b = block(kind, group(-3 * step), far)
        return remote(b, b, f_s.at[stream], f_r.at[stream], at_z(step))

    def y_copy(kind, off):
        slot = NZ if kind == UP else off % NZ
        b = block(kind, group(off), 0)
        return remote(b, b, y_s.at[slot], y_r.at[slot], opposite)

    def c_copy(kind, far, off):
        b = block(kind, group(off), far)
        i = off % NZ
        return remote(b, b, c_s.at[kind, far, i], c_r.at[kind, far, i], sibling)

    def x_copy(slot):
        if slot == 0:
            return remote(inputs, xs.at[tensor], x_s.at[0], x_r.at[0], partner)
        if slot <= 3:
            return remote(inputs, xs.at[tensor], x_s.at[slot], x_r.at[slot], at_x(slot))
        b = xs.at[x * 2 + (1 - yl)]
        return remote(b, b, x_s.at[slot], x_r.at[slot], at_x(slot - 3))

    pre_loads = [
        pltpu.make_async_copy(ref, pre.at[i], loc.at[i])
        for i, ref in enumerate((gate_pre, up_pre, hidden_grad))
    ]
    w_loads = [
        pltpu.make_async_copy(ref, w.at[i], loc.at[3 + i])
        for i, ref in enumerate((gate_weight, up_weight))
    ]
    x_load = pltpu.make_async_copy(inputs, xs.at[tensor], loc.at[5])
    for cp in pre_loads + w_loads + [x_load]:
        cp.start()

    barrier = pltpu.get_barrier_semaphore()
    peers = [at_z(1), at_z(-1), opposite, sibling]
    peers += [{"dp": dp, "tensor": (tensor + i) % NZ} for i in range(1, NZ)]
    for peer in peers:
        pl.semaphore_signal(barrier, inc=1, device_id=peer, device_id_type=MESH)

    for cp in pre_loads:
        cp.wait()

    def elementwise(i, _):
        cols = pl.ds(pl.multiple_of(i * 256, 256), 256)
        gate_value = pre[0, :, cols].astype(jnp.float32)
        up_value = pre[1, :, cols].astype(jnp.float32)
        grad_value = pre[2, :, cols].astype(jnp.float32)
        sig = 1.0 / (1.0 + jnp.exp(-gate_value))
        grads[UP, z, pl.ds(own_rows, ROWS), cols] = (grad_value * gate_value * sig).astype(jnp.bfloat16)
        grads[GATE, z, pl.ds(own_rows, ROWS), cols] = (
            grad_value * up_value * sig * (1.0 + gate_value * (1.0 - sig))
        ).astype(jnp.bfloat16)
        return 0

    lax.fori_loop(0, HID // 256, elementwise, 0)
    pl.semaphore_wait(barrier, len(peers))

    started = []

    def go(cp):
        cp.start()
        started.append(cp)

    def forward(stream, hop):
        if hop < 2:
            for way in (0, 1):
                go(z_copy(way, stream, hop + 1))
        else:
            go(far_copy(stream))

    def arrive_z(stream, hop):
        kind, far = STREAM[stream]
        for way in (0, 1):
            z_copy(way, stream, hop).wait_recv()
            if kind == GATE and hop < 2:
                go(z_copy(way, stream, hop + 1))
        if kind == GATE and hop == 2:
            forward(stream, hop)
        for off in (-(hop + 1), hop + 1):
            if kind == GATE:
                go(y_copy(GATE, off))
            go(c_copy(kind, far, off))

    def arrive_far(stream):
        kind, far = STREAM[stream]
        far_copy(stream).wait_recv()
        if kind == GATE:
            go(y_copy(GATE, 4))
        go(c_copy(kind, far, 4))

    def arrive_y(off):
        y_copy(GATE, off).wait_recv()
        go(c_copy(GATE, 1, off))

    def from_sibling(kind, far, off):
        c_copy(kind, far, off).wait_recv()

    def wgrad(kind, off):
        g = group(off)
        acc = (gate_acc, up_acc)[kind]
        for half in (0, 1):
            cols = pl.ds(half * 896, 896)
            prod = jnp.dot(xt[g], grads[kind, g, :, cols], preferred_element_type=jnp.float32)
            if off != 0:
                prod = acc[:, cols] + prod
            if off == 4:
                prod = prod * SCALE
            acc[:, cols] = prod

    def igrad(off):
        g = group(off)
        part[g] = jnp.dot(grads[GATE, g], wt[GATE], preferred_element_type=jnp.float32)

    def piece(step):
        return pl.ds(pl.multiple_of(((x + step) % NX) * PIECE, PIECE), PIECE)

    def g_copy(off, step):
        i = off % NZ
        return remote(
            part_b.at[group(off), :, piece(step), :], rx.at[i, step - 1],
            g_s.at[i, step - 1], g_r.at[i, step - 1], at_x(step),
        )

    def finish(off):
        g = group(off)
        prod = jnp.dot(grads[UP, g], wt[UP], preferred_element_type=jnp.float32)
        prod = (part[g] + prod).astype(jnp.bfloat16)
        for h in (0, 1):
            part_b[g, h] = prod[h * 128 : (h + 1) * 128]
        for step in (1, 2, 3):
            go(g_copy(off, step))

    def h_copy(off, h):
        return remote(
            sums.at[off % NZ, h], fin.at[tensor, h], h_s.at[off % NZ, h], h_r.at[tensor, h],
            {"dp": dp, "tensor": group(off)},
        )

    def to_owner(off, h, total):
        sums[off % NZ, h] = total.astype(jnp.bfloat16)
        pl.when(tensor != group(off))(lambda: h_copy(off, h).start())

        @pl.when(tensor == group(off))
        def _():
            fin[tensor, h] = total.astype(jnp.bfloat16)

    def collect(off):
        total = part_b[group(off), :, piece(0), :].astype(jnp.float32)
        for step in (1, 2, 3):
            g_copy(off, step).wait_recv()
            total = total + rx[off % NZ, step - 1].astype(jnp.float32)
        for h in (0, 1):
            to_owner(off, h, total[h])

    def last_half(far):
        return 1 - yh if far else yh

    def last_copy(far, step):
        h = last_half(far)
        return remote(
            part_b.at[group(4), h, piece(step), :], rx.at[4, step - 1, h],
            g_s.at[4 + 4 * far, step - 1], g_r.at[4 + 4 * far, step - 1], at_x(step),
        )

    def last_finish(far):
        g, h = group(4), last_half(far)
        rows = pl.ds(pl.multiple_of(h * 128, 128), 128)
        prod = jnp.dot(grads[UP, g, rows, :], wt[UP], preferred_element_type=jnp.float32)
        part_b[g, h] = (part[g, rows, :] + prod).astype(jnp.bfloat16)
        for step in (1, 2, 3):
            go(last_copy(far, step))

    def collect_last(far):
        h = last_half(far)
        total = part_b[group(4), h, piece(0), :].astype(jnp.float32)
        for step in (1, 2, 3):
            last_copy(far, step).wait_recv()
            total = total + rx[4, step - 1, h].astype(jnp.float32)
        to_owner(4, h, total)

    for way in (0, 1):
        go(z_copy(way, 0, 0))
    go(y_copy(UP, 0))
    for way in (0, 1):
        go(z_copy(way, 1, 0))
    go(c_copy(UP, 0, 0))
    go(c_copy(GATE, 0, 0))
    go(x_copy(0))
    go(y_copy(GATE, 0))
    for slot in (1, 2, 3):
        go(x_copy(slot))

    for cp in w_loads:
        cp.wait()

    def flip_w(i, _):
        cols = pl.ds(pl.multiple_of(i * 256, 256), 256)
        for kind in (GATE, UP):
            wt[kind, cols, :] = w[kind, :, cols].T
        return 0

    lax.fori_loop(0, HID // 256, flip_w, 0)

    arrive_z(0, 0)
    y_copy(UP, 0).wait_recv()
    for way in (0, 1):
        go(z_copy(way, 2, 0))
    go(c_copy(UP, 1, 0))
    x_copy(0).wait_recv()
    for slot in (4, 5, 6):
        go(x_copy(slot))
    arrive_z(1, 0)

    x_load.wait()
    for slot in range(1, 7):
        x_copy(slot).wait_recv()

    def flip_x(i, _):
        xt[i] = xs[i].T
        return 0

    lax.fori_loop(0, NZ, flip_x, 0)

    def from_both(kind, off):
        for far in (0, 1):
            from_sibling(kind, far, off)

    def do(kind, off):
        from_both(kind, off)
        if kind == GATE:
            igrad(off)
        else:
            finish(off)
        wgrad(kind, off)

    arrive_y(0)
    arrive_z(0, 1)
    forward(1, 0)
    do(GATE, 0)
    do(UP, 0)
    arrive_y(-1)
    arrive_z(2, 0)
    do(GATE, -1)
    do(UP, -1)
    arrive_y(1)
    arrive_z(0, 2)
    forward(2, 0)
    do(GATE, 1)
    do(UP, 1)
    arrive_y(-2)
    arrive_z(1, 1)
    forward(1, 1)
    collect(0)
    do(GATE, -2)
    arrive_far(0)
    arrive_y(2)
    collect(-1)
    collect(1)
    arrive_z(2, 1)
    forward(2, 1)
    do(GATE, 2)
    arrive_y(-3)
    do(UP, -2)
    do(GATE, -3)
    arrive_z(1, 2)
    forward(1, 2)
    do(UP, 2)
    arrive_y(3)
    arrive_z(2, 2)
    forward(2, 2)
    do(GATE, 3)
    from_both(UP, -3)
    finish(-3)
    arrive_y(4)
    arrive_far(1)
    from_both(UP, 3)
    finish(3)
    collect(-2)
    collect(2)
    from_both(GATE, 4)
    igrad(4)
    from_sibling(UP, 0, 4)
    last_finish(0)
    arrive_far(2)
    wgrad(UP, -3)
    from_sibling(UP, 1, 4)
    last_finish(1)
    collect(-3)
    collect(3)
    wgrad(UP, 3)
    collect_last(0)
    wgrad(GATE, 4)
    for cp in started:
        cp.wait_send()
    collect_last(1)
    wgrad(UP, 4)

    def arrived(i, _):
        @pl.when(i != tensor)
        def _():
            for h in (0, 1):
                remote(fin.at[i, h], fin.at[i, h], h_s.at[0, h], h_r.at[i, h], sibling).wait_recv()

        return 0

    lax.fori_loop(0, NZ, arrived, 0)
    for i in range(NX):
        total = fin[2 * i].astype(jnp.float32) + fin[2 * i + 1].astype(jnp.float32)
        for h in (0, 1):
            igrad_out[h * 128 + i * PIECE : h * 128 + (i + 1) * PIECE, :] = total[h].astype(jnp.bfloat16)

    for off in OFFS:
        @pl.when(tensor != group(off))
        def _():
            for h in (0, 1):
                h_copy(off, h).wait_send()


def write_out(*refs):
    n = len(refs) // 2
    sem = refs[-1]
    copies = []
    for i in range(n):
        rows = refs[i].shape[0] // PARTS
        for j in range(PARTS):
            at = pl.ds(j * rows, rows)
            copies.append(pltpu.make_async_copy(refs[i].at[at, :], refs[n + i].at[at, :], sem.at[i, j]))
    for cp in copies:
        cp.start()
    for cp in copies:
        cp.wait()


def per_device(*args):
    bf16, f32 = jnp.bfloat16, jnp.float32
    dma = pltpu.SemaphoreType.DMA
    hbm = pl.BlockSpec(memory_space=pl.ANY)
    vmem = pl.BlockSpec(memory_space=pltpu.VMEM)
    outs = (((GROUP, FEAT), bf16), ((FEAT, HID), f32), ((FEAT, HID), f32))
    held = pl.pallas_call(
        kernel,
        out_shape=tuple(pltpu.VMEM(*o) for o in outs),
        in_specs=[hbm] * 6,
        out_specs=(vmem,) * 3,
        scratch_shapes=[
            pltpu.VMEM((2, NZ, GROUP, HID), bf16),
            pltpu.VMEM((NZ, GROUP, FEAT), bf16),
            pltpu.VMEM((NZ, FEAT, GROUP), bf16),
            pltpu.VMEM((2, FEAT, HID), bf16),
            pltpu.VMEM((2, HID, FEAT), bf16),
            pltpu.VMEM((NZ, GROUP, FEAT), f32),
            pltpu.VMEM((NZ, 2, 128, FEAT), bf16),
            pltpu.VMEM((NZ, 3, 2, PIECE, FEAT), bf16),
            pltpu.VMEM((NZ, 2, PIECE, FEAT), bf16),
            pltpu.VMEM((NZ, 2, PIECE, FEAT), bf16),
            pltpu.VMEM((3, ROWS, HID), bf16),
            dma((6,)),
            dma((2, 3, 3)), dma((2, 3, 3)),
            dma((3,)), dma((3,)),
            dma((NZ + 1,)), dma((NZ + 1,)),
            dma((2, 2, NZ)), dma((2, 2, NZ)),
            dma((7,)), dma((7,)),
            dma((NZ + 1, 3)), dma((NZ + 1, 3)),
            dma((NZ, 2)), dma((NZ, 2)),
        ],
        compiler_params=pltpu.CompilerParams(
            collective_id=0, has_side_effects=True, vmem_limit_bytes=VMEM_BYTES
        ),
        cost_estimate=pl.CostEstimate(flops=7516192768, bytes_accessed=8 * 2**20, transcendentals=0),
        name="swiglu_bwd",
    )(*args)
    return tuple(
        pl.pallas_call(
            write_out,
            out_shape=tuple(jax.ShapeDtypeStruct(*o) for o in outs),
            in_specs=[hbm] * 3,
            out_specs=(hbm,) * 3,
            scratch_shapes=[dma((3, PARTS))],
            compiler_params=pltpu.CompilerParams(vmem_limit_bytes=4 * 2**20),
            name="write_out",
        )(*held)
    )


def solution(mesh):
    in_specs = (
        P("tensor", "dp"),
        P("dp", "tensor"),
        P("dp", "tensor"),
        P("dp", "tensor"),
        P("dp", "tensor"),
        P("dp", "tensor"),
    )
    out_specs = (P("tensor", "dp"), P("dp", "tensor"), P("dp", "tensor"))
    return jax.shard_map(
        per_device, mesh=mesh, in_specs=in_specs, out_specs=out_specs, check_vma=False
    )
```
